32 devices in a mesh: seq: 8 (over y, x, core), chan: 4 (over z).
Axes of the slice: x: 2, y: 2, z: 4, core: 2. Of those that a mesh axis runs over, the one named last changes fastest.
Arguments:
- out_grad: bfloat16 [4096, 8192], P('seq', 'chan'), may hold values from -6 to 6
- out_weight: bfloat16 [1024, 8192], P(None, 'chan'), may hold values from -0.0625 to 0.0625
- conv_input: bfloat16 [1024, 4096], P('chan', 'seq'), may hold values from -6 to 6
- gate_values: bfloat16 [1024, 4096], P('chan', 'seq'), may hold values from -6 to 6
- conv_output: bfloat16 [1024, 4096], P('chan', 'seq'), may hold values from -6 to 6
- filters: bfloat16 [2, 1024, 512], P(None, 'chan'), may hold values from -0.29882812 to 0.29882812
- filter_reach: int32 [16], replicated, may hold values from 128 to 512, as said below
Outputs:
- grad_input: float32 [1024, 4096], P('chan', 'seq')
- grad_gate: float32 [1024, 4096], P('chan', 'seq')
- grad_weight: float32 [1024, 8192], P('seq', 'chan')
- grad_filters: float32 [2, 1024, 512], P(None, 'chan', 'seq')
The draws below stay inside these ranges and needn't reach their ends.
Inputs may be any that keep to these rules, and one draw needn't show every extreme that they name: `filter_reach`: group g holds channels g * 64 to (g + 1) * 64 - 1. Every reach is a multiple of 128, and at least one group has reach 512.
All inputs are finite; a program needn't handle non-finite values.
Results may differ from the reference program's by a relative error of at most 0.014.
Values may be sent and summed in bfloat16 or wider, within the bound.
A program may use at most 128 MiB of HBM per device.

```python
import jax
import jax.numpy as jnp
from jax import lax

D = 8192
C = 1024
GROUP = 64
TAPS = 512
TOKENS = 4096
N_CHAN = 4


def draw_filter_reach(key, part):
    levels = TAPS // 128
    groups_total = C // GROUP
    key_multiples, second = jax.random.split(jax.random.fold_in(key, 17))
    multiples = jax.random.randint(key_multiples, (groups_total,), 1, levels + 1)
    chosen = jax.random.randint(second, (), 0, groups_total)
    picked = jnp.where(jnp.arange(groups_total) == chosen, levels, multiples)
    return (128 * picked).astype(jnp.int32)


def block_levels(own_key, dims, pieces, low, largest):
    factor_of, own = 1.0, jax.random.fold_in(own_key, 6)
    for axis_at, parts in pieces:
        heights = jnp.exp(jax.random.uniform(jax.random.fold_in(own, axis_at), (parts,), jnp.float32, low / len(pieces), largest / len(pieces)))
        factor_of = factor_of * jnp.repeat(heights, dims[axis_at] // parts).reshape([-1 if axis == axis_at else 1 for axis in range(len(dims))])
    return factor_of


def scatter_about(own_key, shape, scale, limit, pieces=(), held_as=jnp.bfloat16):
    entries = scale * jax.random.normal(own_key, shape, jnp.float32)
    if pieces:
        entries = entries * block_levels(own_key, shape, pieces, -0.22, 0.18)
    return jnp.clip(entries, -limit, limit).astype(held_as)


def setup_inputs(seed: int = 0) -> dict:
    key_list = jax.random.split(jax.random.key(seed), 8)
    out_grad = scatter_about(key_list[0], (TOKENS, D), 1.0, 6.0, ((0, 8), (1, 4)))
    out_weight = scatter_about(key_list[1], (C, D), D ** -0.5, 0.0625, ((1, 4),))
    conv_input = scatter_about(key_list[2], (C, TOKENS), 1.0, 6.0, ((0, 4), (1, 8)))
    gate_values = scatter_about(key_list[3], (C, TOKENS), 1.0, 6.0, ((0, 4), (1, 8)))
    conv_output = scatter_about(key_list[4], (C, TOKENS), 1.0, 6.0, ((0, 4), (1, 8)))
    filters = scatter_about(key_list[5], (2, C, TAPS), 0.05, 0.29882812, ((1, 4),))
    filter_reach = draw_filter_reach(jax.random.fold_in(key_list[7], 71), 0)
    return {"out_grad": out_grad, "out_weight": out_weight, "conv_input": conv_input, "gate_values": gate_values, "conv_output": conv_output, "filters": filters, "filter_reach": filter_reach}


def reference(out_grad, out_weight, conv_input, gate_values, conv_output, filters, filter_reach):
    feature_block = D // N_CHAN
    grad_gated = jnp.zeros((C, TOKENS), jnp.float32)
    for portion in range(N_CHAN):
        weight_cols = out_weight[:, portion * feature_block:(portion + 1) * feature_block]
        grad_cols = out_grad[:, portion * feature_block:(portion + 1) * feature_block]
        partial_value = jnp.dot(weight_cols, grad_cols.T, preferred_element_type=jnp.float32)
        rounded = lax.optimization_barrier(partial_value.astype(jnp.bfloat16))
        grad_gated = grad_gated + rounded.astype(jnp.float32)
    grad_scale = 1.0 / (TOKENS ** 0.5)
    gated = (conv_output.astype(jnp.float32) * gate_values.astype(jnp.float32)).astype(jnp.bfloat16)
    grad_weight = jnp.dot(gated, out_grad, preferred_element_type=jnp.float32) * grad_scale
    grad_gate = grad_gated * conv_output.astype(jnp.float32)
    grad_conv = (grad_gated * gate_values.astype(jnp.float32)).astype(jnp.bfloat16)
    channel_reach = filter_reach[jnp.arange(C, dtype=jnp.int32) // GROUP]
    inside = jnp.arange(TAPS, dtype=jnp.int32)[None, :] < channel_reach[:, None]
    forward_taps = jnp.where(inside, filters[0], jnp.zeros((), filters.dtype)).astype(jnp.float32)
    backward_taps = jnp.where(inside, filters[1], jnp.zeros((), filters.dtype)).astype(jnp.float32)
    shifted_back = jnp.pad(backward_taps, ((0, 0), (1, 0)))
    fft_len = TOKENS + 2 * TAPS
    grad_spec = jnp.fft.rfft(grad_conv.astype(jnp.float32), n=fft_len, axis=1)
    input_spec = jnp.fft.rfft(conv_input.astype(jnp.float32), n=fft_len, axis=1)
    ahead_spec = jnp.fft.rfft(forward_taps, n=fft_len, axis=1)
    behind_spec = jnp.fft.rfft(shifted_back, n=fft_len, axis=1)
    grad_input = jnp.fft.irfft(grad_spec * jnp.conj(ahead_spec), n=fft_len, axis=1)[:, :TOKENS]
    grad_input = grad_input + jnp.fft.irfft(grad_spec * behind_spec, n=fft_len, axis=1)[:, :TOKENS]
    ahead_grad = jnp.fft.irfft(grad_spec * jnp.conj(input_spec), n=fft_len, axis=1)[:, :TAPS]
    behind_grad = jnp.fft.irfft(jnp.conj(grad_spec) * input_spec, n=fft_len, axis=1)[:, 1:TAPS + 1]
    grad_filters = jnp.stack([ahead_grad, behind_grad]) * inside[None].astype(ahead_grad.dtype) * grad_scale
    return grad_input, grad_gate, grad_weight, grad_filters
```

```python
import math

import jax
import jax.numpy as jnp
from jax import lax
from jax.experimental import pallas as pl
from jax.experimental.pallas import tpu as pltpu
from jax.sharding import PartitionSpec as P

GROUP = 64
LANES = 128
STEP = 8


def extended(block, sides, width):
    for axis, dim in sides:
        count = lax.axis_size(axis)
        forward = [(i, i + 1) for i in range(count - 1)]
        backward = [(target, source) for source, target in forward]
        low = lax.ppermute(
            lax.slice_in_dim(block, block.shape[dim] - width, None, axis=dim), axis, forward
        )
        high = lax.ppermute(lax.slice_in_dim(block, 0, width, axis=dim), axis, backward)
        block = jnp.concatenate([low, block, high], axis=dim)
    return block


def correlate_kernel(grad_ref, taps_ref, input_ref, out_ref, tiles_ref, lines_ref):
    channels = grad_ref.shape[0]
    span, tok_len = taps_ref.shape[1], input_ref.shape[1]
    out_blocks, tap_blocks = tok_len // LANES, span // LANES
    tile_count = tiles_ref.shape[1] // LANES
    row = lax.broadcasted_iota(jnp.int32, (LANES, LANES), 0)
    lane = lax.broadcasted_iota(jnp.int32, (LANES, LANES), 1)
    first = lane <= row
    rows = out_ref.shape[1]

    @pl.when(pl.program_id(0) == 0)
    def _():
        lines_ref[...] = jnp.zeros_like(lines_ref)

    for pair in range(channels // 2):
        for half in range(2):
            channel = 2 * pair + half

            def rolled(window):
                line = grad_ref[channel : channel + 1, window * LANES : (window + 1) * LANES]
                spread = jnp.broadcast_to(line, (LANES, LANES))
                return pltpu.roll(spread, 1, 1, stride=1, stride_axis=0)

            current = rolled(0)
            for tile in range(tile_count):
                following = rolled(tile + 1)
                tiles_ref[
                    pair % 2, tile * LANES : (tile + 1) * LANES, half * LANES : (half + 1) * LANES
                ] = jnp.where(first, current, following).astype(jnp.bfloat16)
                current = following
            top = half * rows
            for a in range(out_blocks):
                lines_ref[pair % 2, top + a : top + a + 1, a * LANES : a * LANES + span] = taps_ref[
                    channel : channel + 1, :
                ]
            top = top + out_blocks
            for b in range(tap_blocks):
                lines_ref[pair % 2, top + b : top + b + 1, b * LANES : b * LANES + tok_len] = (
                    input_ref[channel : channel + 1, :]
                )
        product = jnp.dot(
            lines_ref[pair % 2].astype(jnp.bfloat16),
            tiles_ref[pair % 2],
            preferred_element_type=jnp.float32,
        )
        out_ref[2 * pair] = product[:rows, :LANES]
        out_ref[2 * pair + 1] = product[rows:, LANES:]


def filter_terms(grad_ext, conv_input, kernel_taps):
    channels, tok_len = conv_input.shape
    span = kernel_taps.shape[1]
    out_blocks = tok_len // LANES
    tap_blocks = span // LANES
    tile_count = out_blocks + tap_blocks - 1
    depth = tile_count * LANES
    rows = -(-(out_blocks + tap_blocks) // 16) * 16

    def turned(array):
        return array.reshape(channels, -1, LANES)[:, :, ::-1].reshape(channels, -1).astype(jnp.float32)

    out = pl.pallas_call(
        correlate_kernel,
        grid=(channels // STEP,),
        out_shape=jax.ShapeDtypeStruct((channels, rows, LANES), jnp.float32),
        in_specs=[
            pl.BlockSpec((STEP, grad_ext.shape[1]), lambda i: (i, 0)),
            pl.BlockSpec((STEP, span), lambda i: (i, 0)),
            pl.BlockSpec((STEP, tok_len), lambda i: (i, 0)),
        ],
        out_specs=pl.BlockSpec((STEP, rows, LANES), lambda i: (i, 0, 0)),
        scratch_shapes=[
            pltpu.VMEM((2, depth, 2 * LANES), jnp.bfloat16),
            pltpu.VMEM((2, 2 * rows, depth), jnp.float32),
        ],
        compiler_params=pltpu.CompilerParams(vmem_limit_bytes=24 * 1024 * 1024),
        cost_estimate=pl.CostEstimate(
            flops=2 * 2 * rows * 2 * LANES * depth * channels,
            bytes_accessed=4 * channels * (depth + 2 * span + rows * LANES),
            transcendentals=0,
        ),
    )(grad_ext.astype(jnp.float32), turned(kernel_taps), turned(conv_input))
    result = out[:, :out_blocks].reshape(channels, tok_len)
    tap_sums = out[:, out_blocks : out_blocks + tap_blocks].reshape(channels, span)
    return result, tap_sums


def on_device(out_grad, out_weight, conv_input, gate_values, conv_output, filters, filter_reach):
    chan_rows = conv_input.shape[0]
    tok_len = conv_input.shape[1]
    tap_count = filters.shape[2]
    gated = (conv_output.astype(jnp.float32) * gate_values.astype(jnp.float32)).astype(jnp.bfloat16)
    gathered = lax.all_gather(gated, "chan", axis=0, tiled=True)
    partial = lax.dot_general(
        out_weight, out_grad, (((1,), (1,)), ((), ())), preferred_element_type=jnp.float32
    ).astype(jnp.bfloat16)
    partial, gathered = lax.optimization_barrier((partial, gathered))
    summed = lax.psum_scatter(partial, "chan", scatter_dimension=0, tiled=True)
    weight_term = jnp.dot(gathered, out_grad, preferred_element_type=jnp.float32)
    summed, weight_term = lax.optimization_barrier((summed, weight_term))
    grad_gated = summed.astype(jnp.float32)
    grad_gate = grad_gated * conv_output.astype(jnp.float32)
    grad_conv = (grad_gated * gate_values.astype(jnp.float32)).astype(jnp.bfloat16)
    grad_ext = extended(grad_conv, (("seq", 1),), tap_count)
    channel_ids = lax.axis_index("chan") * chan_rows + jnp.arange(chan_rows, dtype=jnp.int32)
    group_ids = channel_ids // GROUP
    levels = jnp.arange(filter_reach.shape[0], dtype=jnp.int32)
    reach_rows = jnp.sum(
        jnp.where(group_ids[:, None] == levels[None, :], filter_reach[None, :], 0), axis=1
    )
    inside = jnp.arange(tap_count, dtype=jnp.int32)[None, :] < reach_rows[:, None]
    nothing = jnp.zeros((), filters.dtype)
    ahead = jnp.where(inside, filters[0], nothing)
    behind = jnp.where(inside, filters[1], nothing)
    kernel_taps = jnp.concatenate([behind[:, ::-1], ahead], axis=1)
    grad_input, tap_sums = filter_terms(grad_ext, conv_input, kernel_taps)
    tap_grads = jnp.stack([tap_sums[:, tap_count:], tap_sums[:, :tap_count][:, ::-1]])
    tap_grads = tap_grads * inside[None].astype(jnp.float32)
    grad_scale = 1.0 / math.sqrt(tok_len * lax.axis_size("seq"))
    weight_sum, taps_sum = (
        lax.psum_scatter(weight_term, "seq", scatter_dimension=0, tiled=True),
        lax.psum_scatter(tap_grads, "seq", scatter_dimension=2, tiled=True),
    )
    return (grad_input, grad_gate, weight_sum * grad_scale, taps_sum * grad_scale)


def solution(mesh):
    return jax.shard_map(
        on_device,
        mesh=mesh,
        in_specs=(
            P("seq", "chan"),
            P(None, "chan"),
            P("chan", "seq"),
            P("chan", "seq"),
            P("chan", "seq"),
            P(None, "chan", None),
            P(),
        ),
        out_specs=(P("chan", "seq"), P("chan", "seq"), P("seq", "chan"), P(None, "chan", "seq")),
        check_vma=False,
    )
```

```python
import math

import jax
import jax.numpy as jnp
from jax import lax
from jax.experimental import pallas as pl
from jax.experimental.pallas import tpu as pltpu
from jax.sharding import PartitionSpec as P

GROUP = 64
LANES = 128
STEP = 8


def extended(block, sides, width):
    for axis, dim in sides:
        count = lax.axis_size(axis)
        forward = [(i, i + 1) for i in range(count - 1)]
        backward = [(target, source) for source, target in forward]
        low = lax.ppermute(
            lax.slice_in_dim(block, block.shape[dim] - width, None, axis=dim), axis, forward
        )
        high = lax.ppermute(lax.slice_in_dim(block, 0, width, axis=dim), axis, backward)
        block = jnp.concatenate([low, block, high], axis=dim)
    return block


def correlate_kernel(grad_ref, taps_ref, input_ref, out_ref, tiles_ref, lines_ref):
    channels = grad_ref.shape[0]
    span, tok_len = taps_ref.shape[1], input_ref.shape[1]
    out_blocks, tap_blocks = tok_len // LANES, span // LANES
    tile_count = tiles_ref.shape[1] // LANES
    row = lax.broadcasted_iota(jnp.int32, (LANES, LANES), 0)
    lane = lax.broadcasted_iota(jnp.int32, (LANES, LANES), 1)
    first = lane <= row
    rows = out_ref.shape[1]

    @pl.when(pl.program_id(0) == 0)
    def _():
        lines_ref[...] = jnp.zeros_like(lines_ref)

    for pair in range(channels // 2):
        for half in range(2):
            channel = 2 * pair + half

            def rolled(window):
                line = grad_ref[channel : channel + 1, window * LANES : (window + 1) * LANES]
                spread = jnp.broadcast_to(line, (LANES, LANES))
                return pltpu.roll(spread, 1, 1, stride=1, stride_axis=0)

            current = rolled(0)
            for tile in range(tile_count):
                following = rolled(tile + 1)
                tiles_ref[
                    pair % 2, tile * LANES : (tile + 1) * LANES, half * LANES : (half + 1) * LANES
                ] = jnp.where(first, current, following).astype(jnp.bfloat16)
                current = following
            top = half * rows
            for a in range(out_blocks):
                lines_ref[pair % 2, top + a : top + a + 1, a * LANES : a * LANES + span] = taps_ref[
                    channel : channel + 1, :
                ]
            top = top + out_blocks
            for b in range(tap_blocks):
                lines_ref[pair % 2, top + b : top + b + 1, b * LANES : b * LANES + tok_len] = (
                    input_ref[channel : channel + 1, :]
                )
        product = jnp.dot(
            lines_ref[pair % 2].astype(jnp.bfloat16),
            tiles_ref[pair % 2],
            preferred_element_type=jnp.float32,
        )
        out_ref[2 * pair] = product[:rows, :LANES]
        out_ref[2 * pair + 1] = product[rows:, LANES:]


def filter_terms(grad_ext, conv_input, kernel_taps):
    channels, tok_len = conv_input.shape
    span = kernel_taps.shape[1]
    out_blocks = tok_len // LANES
    tap_blocks = span // LANES
    tile_count = out_blocks + tap_blocks - 1
    depth = tile_count * LANES
    rows = -(-(out_blocks + tap_blocks) // 16) * 16

    def turned(array):
        return array.reshape(channels, -1, LANES)[:, :, ::-1].reshape(channels, -1).astype(jnp.float32)

    out = pl.pallas_call(
        correlate_kernel,
        grid=(channels // STEP,),
        out_shape=jax.ShapeDtypeStruct((channels, rows, LANES), jnp.float32),
        in_specs=[
            pl.BlockSpec((STEP, grad_ext.shape[1]), lambda i: (i, 0)),
            pl.BlockSpec((STEP, span), lambda i: (i, 0)),
            pl.BlockSpec((STEP, tok_len), lambda i: (i, 0)),
        ],
        out_specs=pl.BlockSpec((STEP, rows, LANES), lambda i: (i, 0, 0)),
        scratch_shapes=[
            pltpu.VMEM((2, depth, 2 * LANES), jnp.bfloat16),
            pltpu.VMEM((2, 2 * rows, depth), jnp.float32),
        ],
        compiler_params=pltpu.CompilerParams(vmem_limit_bytes=24 * 1024 * 1024),
        cost_estimate=pl.CostEstimate(
            flops=8 * LANES * LANES * depth * channels,
            bytes_accessed=4 * channels * (depth + 2 * span + rows * LANES),
            transcendentals=0,
        ),
    )(grad_ext.astype(jnp.float32), turned(kernel_taps), turned(conv_input))
    result = out[:, :out_blocks].reshape(channels, tok_len)
    tap_sums = out[:, out_blocks : out_blocks + tap_blocks].reshape(channels, span)
    return result, tap_sums


def on_device(out_grad, out_weight, conv_input, gate_values, conv_output, filters, filter_reach):
    chan_rows = conv_input.shape[0]
    tok_len = conv_input.shape[1]
    tap_count = filters.shape[2]
    gated = (conv_output.astype(jnp.float32) * gate_values.astype(jnp.float32)).astype(jnp.bfloat16)
    gathered = lax.all_gather(gated, "chan", axis=0, tiled=True)
    partial = lax.dot_general(
        out_weight, out_grad, (((1,), (1,)), ((), ())), preferred_element_type=jnp.float32
    ).astype(jnp.bfloat16)
    partial, gathered = lax.optimization_barrier((partial, gathered))
    summed = lax.psum_scatter(partial, "chan", scatter_dimension=0, tiled=True)
    weight_term = jnp.dot(gathered, out_grad, preferred_element_type=jnp.float32).astype(jnp.bfloat16)
    summed, weight_term = lax.optimization_barrier((summed, weight_term))
    weight_sum = lax.psum_scatter(weight_term, "seq", scatter_dimension=0, tiled=True)
    grad_gated = summed.astype(jnp.float32)
    grad_gate = grad_gated * conv_output.astype(jnp.float32)
    grad_conv = (grad_gated * gate_values.astype(jnp.float32)).astype(jnp.bfloat16)
    grad_ext = extended(grad_conv, (("seq", 1),), tap_count)
    channel_ids = lax.axis_index("chan") * chan_rows + jnp.arange(chan_rows, dtype=jnp.int32)
    group_ids = channel_ids // GROUP
    levels = jnp.arange(filter_reach.shape[0], dtype=jnp.int32)
    reach_rows = jnp.sum(
        jnp.where(group_ids[:, None] == levels[None, :], filter_reach[None, :], 0), axis=1
    )
    inside = jnp.arange(tap_count, dtype=jnp.int32)[None, :] < reach_rows[:, None]
    nothing = jnp.zeros((), filters.dtype)
    ahead = jnp.where(inside, filters[0], nothing)
    behind = jnp.where(inside, filters[1], nothing)
    kernel_taps = jnp.concatenate([behind[:, ::-1], ahead], axis=1)
    grad_input, tap_sums = filter_terms(grad_ext, conv_input, kernel_taps)
    tap_grads = jnp.stack([tap_sums[:, tap_count:], tap_sums[:, :tap_count][:, ::-1]])
    tap_grads = tap_grads * inside[None].astype(jnp.float32)
    grad_scale = 1.0 / math.sqrt(tok_len * lax.axis_size("seq"))
    tap_grads, weight_sum, grad_input = lax.optimization_barrier(
        (tap_grads.astype(jnp.bfloat16), weight_sum, grad_input)
    )
    taps_sum = lax.psum_scatter(tap_grads, "seq", scatter_dimension=2, tiled=True)
    weight_sum, taps_sum = weight_sum.astype(jnp.float32), taps_sum.astype(jnp.float32)
    return (grad_input, grad_gate, weight_sum * grad_scale, taps_sum * grad_scale)


def solution(mesh):
    return jax.shard_map(
        on_device,
        mesh=mesh,
        in_specs=(
            P("seq", "chan"),
            P(None, "chan"),
            P("chan", "seq"),
            P("chan", "seq"),
            P("chan", "seq"),
            P(None, "chan", None),
            P(),
        ),
        out_specs=(P("chan", "seq"), P("chan", "seq"), P("seq", "chan"), P(None, "chan", "seq")),
        check_vma=False,
    )
```

```python
import math

import jax
import jax.numpy as jnp
from jax import lax
from jax.experimental import pallas as pl
from jax.experimental.pallas import tpu as pltpu
from jax.sharding import PartitionSpec as P

GROUP = 64
LANES = 128
STEP = 8


def extended(block, sides, width):
    for axis, dim in sides:
        count = lax.axis_size(axis)
        forward = [(i, i + 1) for i in range(count - 1)]
        backward = [(target, source) for source, target in forward]
        low = lax.ppermute(
            lax.slice_in_dim(block, block.shape[dim] - width, None, axis=dim), axis, forward
        )
        high = lax.ppermute(lax.slice_in_dim(block, 0, width, axis=dim), axis, backward)
        block = jnp.concatenate([low, block, high], axis=dim)
    return block


def gather_rows(block, axis):
    count, me = lax.axis_size(axis), lax.axis_index(axis)
    rows = block.shape[0]
    whole = jnp.zeros((count * rows, block.shape[1]), block.dtype)
    whole = lax.dynamic_update_slice(whole, block, (me * rows, 0))
    for step in range(1, count):
        arrived = lax.ppermute(block, axis, [(i, (i + step) % count) for i in range(count)])
        owner = lax.rem(me + count - step, count)
        whole = lax.dynamic_update_slice(whole, arrived, (owner * rows, 0))
    return whole


def turned(array):
    channels = array.shape[0]
    return array.reshape(channels, -1, LANES)[:, :, ::-1].reshape(channels, -1)


def pieces_reversed(array, width):
    total = array.shape[1]
    return jnp.concatenate(
        [array[:, total - start - width : total - start] for start in range(0, total, width)], axis=1
    )


def correlate_kernel(grad_ref, taps_ref, input_ref, out_ref, tiles_ref, lines_ref):
    channels = grad_ref.shape[0]
    span, tok_len = taps_ref.shape[1], input_ref.shape[1]
    out_blocks, tap_blocks = tok_len // LANES, span // LANES
    tile_count = tiles_ref.shape[1] // LANES
    row = lax.broadcasted_iota(jnp.int32, (LANES, LANES), 0)
    lane = lax.broadcasted_iota(jnp.int32, (LANES, LANES), 1)
    first = lane <= row
    rows = out_ref.shape[1]

    @pl.when(pl.program_id(0) == 0)
    def _():
        lines_ref[...] = jnp.zeros_like(lines_ref)

    for pair in range(channels // 2):
        for half in range(2):
            channel = 2 * pair + half

            def rolled(window):
                line = grad_ref[channel : channel + 1, window * LANES : (window + 1) * LANES]
                spread = jnp.broadcast_to(line, (LANES, LANES))
                return pltpu.roll(spread, 1, 1, stride=1, stride_axis=0)

            current = rolled(0)
            for tile in range(tile_count):
                following = rolled(tile + 1)
                tiles_ref[
                    pair % 2, tile * LANES : (tile + 1) * LANES, half * LANES : (half + 1) * LANES
                ] = jnp.where(first, current, following).astype(jnp.bfloat16)
                current = following
            top = half * rows
            for a in range(out_blocks):
                lines_ref[pair % 2, top + a : top + a + 1, a * LANES : a * LANES + span] = taps_ref[
                    channel : channel + 1, :
                ]
            top = top + out_blocks
            for b in range(tap_blocks):
                lines_ref[pair % 2, top + b : top + b + 1, b * LANES : b * LANES + tok_len] = (
                    input_ref[channel : channel + 1, :]
                )
        product = jnp.dot(
            lines_ref[pair % 2].astype(jnp.bfloat16),
            tiles_ref[pair % 2],
            preferred_element_type=jnp.float32,
        )
        out_ref[2 * pair] = product[:rows, :LANES]
        out_ref[2 * pair + 1] = product[rows:, LANES:]


def filter_terms(grad_ext, input_turned, taps_turned):
    channels, tok_len = input_turned.shape
    span = taps_turned.shape[1]
    out_blocks = tok_len // LANES
    tap_blocks = span // LANES
    tile_count = out_blocks + tap_blocks - 1
    depth = tile_count * LANES
    rows = -(-(out_blocks + tap_blocks) // 16) * 16

    out = pl.pallas_call(
        correlate_kernel,
        grid=(channels // STEP,),
        out_shape=jax.ShapeDtypeStruct((channels, rows, LANES), jnp.float32),
        in_specs=[
            pl.BlockSpec((STEP, grad_ext.shape[1]), lambda i: (i, 0)),
            pl.BlockSpec((STEP, span), lambda i: (i, 0)),
            pl.BlockSpec((STEP, tok_len), lambda i: (i, 0)),
        ],
        out_specs=pl.BlockSpec((STEP, rows, LANES), lambda i: (i, 0, 0)),
        scratch_shapes=[
            pltpu.VMEM((2, depth, 2 * LANES), jnp.bfloat16),
            pltpu.VMEM((2, 2 * rows, depth), jnp.float32),
        ],
        compiler_params=pltpu.CompilerParams(vmem_limit_bytes=24 * 1024 * 1024),
        cost_estimate=pl.CostEstimate(
            flops=8 * LANES * LANES * depth * channels,
            bytes_accessed=4 * channels * (depth + 2 * span + rows * LANES),
            transcendentals=0,
        ),
    )(grad_ext.astype(jnp.float32), taps_turned, input_turned)
    result = out[:, :out_blocks].reshape(channels, tok_len)
    tap_sums = out[:, out_blocks : out_blocks + tap_blocks].reshape(channels, span)
    return result, tap_sums


def on_device(out_grad, out_weight, conv_input, gate_values, conv_output, filters, filter_reach):
    chan_rows = conv_input.shape[0]
    tok_len = conv_input.shape[1]
    tap_count = filters.shape[2]
    gated = (conv_output.astype(jnp.float32) * gate_values.astype(jnp.float32)).astype(jnp.bfloat16)
    partial = lax.dot_general(
        out_weight, out_grad, (((1,), (1,)), ((), ())), preferred_element_type=jnp.float32
    ).astype(jnp.bfloat16)
    partial, gated = lax.optimization_barrier((partial, gated))
    summed = lax.psum_scatter(partial, "chan", scatter_dimension=0, tiled=True)
    gathered = gather_rows(gated, "chan")
    weight_term = jnp.dot(gathered, out_grad, preferred_element_type=jnp.float32).astype(jnp.bfloat16)
    summed, weight_term = lax.optimization_barrier((summed, weight_term))
    weight_sum = lax.psum_scatter(weight_term, "seq", scatter_dimension=0, tiled=True)
    grad_gated = summed.astype(jnp.float32)
    grad_gate = grad_gated * conv_output.astype(jnp.float32)
    grad_conv = (grad_gated * gate_values.astype(jnp.float32)).astype(jnp.bfloat16)
    grad_ext = extended(grad_conv, (("seq", 1),), tap_count)
    channel_ids = lax.axis_index("chan") * chan_rows + jnp.arange(chan_rows, dtype=jnp.int32)
    group_ids = channel_ids // GROUP
    levels = jnp.arange(filter_reach.shape[0], dtype=jnp.int32)
    reach_rows = jnp.sum(
        jnp.where(group_ids[:, None] == levels[None, :], filter_reach[None, :], 0), axis=1
    )
    inside = jnp.arange(tap_count, dtype=jnp.int32)[None, :] < reach_rows[:, None]
    nothing = jnp.zeros((), filters.dtype)
    ahead = jnp.where(inside, filters[0], nothing)
    behind = jnp.where(inside, filters[1], nothing)
    taps_turned = jnp.concatenate([pieces_reversed(behind, LANES), turned(ahead)], axis=1)
    grad_input, tap_sums = filter_terms(
        grad_ext, turned(conv_input).astype(jnp.float32), taps_turned.astype(jnp.float32)
    )
    width = tap_count // lax.axis_size("seq")
    tap_grads = jnp.stack([tap_sums[:, tap_count:], pieces_reversed(tap_sums[:, :tap_count], width)])
    grad_scale = 1.0 / math.sqrt(tok_len * lax.axis_size("seq"))
    tap_grads, weight_sum, grad_input = lax.optimization_barrier(
        (tap_grads.astype(jnp.bfloat16), weight_sum, grad_input)
    )
    taps_sum = lax.psum_scatter(tap_grads, "seq", scatter_dimension=2, tiled=True)
    weight_sum, taps_sum = weight_sum.astype(jnp.float32), taps_sum.astype(jnp.float32)
    own_taps = lax.axis_index("seq") * width + jnp.arange(width, dtype=jnp.int32)
    taps_sum = jnp.where(
        own_taps[None, None, :] < reach_rows[None, :, None],
        jnp.stack([taps_sum[0], taps_sum[1][:, ::-1]]),
        0.0,
    )
    return (grad_input, grad_gate, weight_sum * grad_scale, taps_sum * grad_scale)


def solution(mesh):
    return jax.shard_map(
        on_device,
        mesh=mesh,
        in_specs=(
            P("seq", "chan"),
            P(None, "chan"),
            P("chan", "seq"),
            P("chan", "seq"),
            P("chan", "seq"),
            P(None, "chan", None),
            P(),
        ),
        out_specs=(P("chan", "seq"), P("chan", "seq"), P("seq", "chan"), P(None, "chan", "seq")),
        check_vma=False,
    )
```
